512 devices in a mesh: slab: 64 (over z_lo, y, core), lev: 8 (over x, z_hi).
Axes of the slice: x: 4, y: 8, z: 8 (z_hi: 2, z_lo: 4; z = z_hi * 4 + z_lo), core: 2. Of those that a mesh axis runs over, the one named last changes fastest.
Arguments:
- fields: float32 [8, 4, 2048, 2048], P('lev', None, 'slab'), may hold values from -6 to 6
- density: float32 [8], P('lev'), may hold values from 0.3 to 1.2
- inv_thickness: float32 [8], P('lev'), may hold values from 2 to 8
Outputs:
- coarse_fields: float32 [8, 4, 512, 512], P('lev', None, 'slab')
- fluxes: float32 [8, 4, 512, 512], P('lev', None, 'slab')
- tendency: float32 [8, 3, 512, 512], P('lev', None, 'slab')
The draws below stay inside these ranges and needn't reach their ends.
All inputs are finite; a program needn't handle non-finite values.
Results may differ from the reference program's by a relative error of at most 0.0003.
Values sent between devices are 32-bit elements; how exact they have to be, the bound alone decides.
A program may use at most 64 MiB of HBM per device.

```python
import math
import jax
import jax.numpy as jnp
from jax import lax

GRID = 2048
TARGET = 512
LEVELS = 8


def block_levels(own_key, extent, shards, smallest, largest):
    loudness, own = 1.0, jax.random.fold_in(own_key, 6)
    for dim, shards_of in shards:
        heights = jnp.exp(jax.random.uniform(jax.random.fold_in(own, dim), (shards_of,), jnp.float32, smallest / len(shards), largest / len(shards)))
        loudness = loudness * jnp.repeat(heights, extent[dim] // shards_of).reshape([-1 if axis == dim else 1 for axis in range(len(extent))])
    return loudness


def scatter_about(key, dims, scale, limit, shards=(), kind=jnp.bfloat16):
    gain = block_levels(key, dims, shards, -0.22, 0.18) if shards else 1.0
    drawn = jax.random.normal(key, dims, jnp.float32) * scale * gain
    return jnp.minimum(jnp.maximum(drawn, -limit), limit).astype(kind)


def setup_inputs(seed: int = 0) -> dict:
    streams_of = jax.random.split(jax.random.key(seed), 4)
    return {
        "fields": scatter_about(streams_of[0], (LEVELS, 4, GRID, GRID), 1.0, 6.0, ((0, 8), (2, 64)), jnp.float32),
        "density": jnp.clip(jnp.exp(math.log(1.2) - 1.3862944 * jax.random.uniform(streams_of[1], (LEVELS,), jnp.float32) ** block_levels(streams_of[1], (LEVELS,), ((0, 8),), -0.2, 0.2)), 0.3, 1.2),
        "inv_thickness": jnp.clip(jnp.exp(math.log(8.0) - 1.3862944 * jax.random.uniform(streams_of[2], (LEVELS,), jnp.float32) ** block_levels(streams_of[2], (LEVELS,), ((0, 8),), -0.2, 0.2)), 2.0, 8.0),
    }


def coarse_one(field_grid):
    spectrum = jnp.fft.rfft2(field_grid)
    kept = TARGET // 2 - 1
    lower = spectrum[:kept + 1, :kept + 1]
    upper = spectrum[GRID - kept:, :kept + 1]
    middle = jnp.zeros((1, kept + 1), spectrum.dtype)
    retained = jnp.concatenate([lower, middle, upper], axis=0)
    retained = jnp.pad(retained, ((0, 0), (0, 1)))
    scale_factor = (TARGET * TARGET) / (GRID * GRID)
    return jnp.fft.irfft2(retained, s=(TARGET, TARGET)) * scale_factor


def one_level(level_fields):
    east_wind, north_wind, vertical_wind, potential_temp = level_fields[0], level_fields[1], level_fields[2], level_fields[3]
    fine_fields = jnp.stack([east_wind, north_wind, vertical_wind, potential_temp,
                             east_wind * vertical_wind, north_wind * vertical_wind,
                             potential_temp * vertical_wind, east_wind * north_wind])
    return lax.map(coarse_one, fine_fields).astype(level_fields.dtype)


def reference(fields, density, inv_thickness):
    coarse_all = lax.map(one_level, fields)
    coarse_fields = coarse_all[:, :4]
    c_east, c_north, c_vert, c_temp = coarse_all[:, 0], coarse_all[:, 1], coarse_all[:, 2], coarse_all[:, 3]
    resolved = jnp.stack([c_east * c_vert, c_north * c_vert, c_temp * c_vert, c_east * c_north], axis=1)
    fluxes = coarse_all[:, 4:] - resolved
    weighted = density[:, None, None, None] * fluxes[:, :3]
    padded = jnp.pad(weighted, ((1, 1), (0, 0), (0, 0), (0, 0)))
    factor = inv_thickness / (2.0 * density)
    tendency = -(padded[2:] - padded[:-2]) * factor[:, None, None, None]
    return coarse_fields, fluxes, tendency
```

```python
import functools

import jax
import jax.numpy as jnp
import ml_dtypes
import numpy as np
from jax import lax
from jax.experimental import pallas as pl
from jax.experimental.pallas import tpu as pltpu
from jax.sharding import PartitionSpec as P

GRID = 2048
TARGET = 512
ORDER = (2, 1, 3, 0)
F32 = jnp.float32
BF16 = jnp.bfloat16


def tables():
    k = np.arange(1, TARGET // 2, dtype=np.float64)
    offsets = np.arange(GRID, dtype=np.float64)
    profile = (1.0 + 2.0 * np.cos(2.0 * np.pi * np.outer(offsets, k) / GRID).sum(1)) / GRID
    index = (GRID // TARGET * np.arange(TARGET)[:, None] - np.arange(GRID)[None, :]) % GRID
    matrix = profile[index].astype(np.float32)
    columns = np.ascontiguousarray(matrix[:128].T)
    first = matrix[:, :512].reshape(4, 8, 2, 8, 8, 2, 32)
    rows = [
        np.stack([first[:, :, c, :, :, core] for c in (1 - core, core)], axis=1).reshape(4, 128, 256)
        for core in range(2)
    ]
    return columns, np.stack(rows)


def split(value):
    high = value.astype(BF16)
    return high, (value - high.astype(F32)).astype(BF16)


def dot(a, b):
    return jnp.dot(a, b, preferred_element_type=F32)


def kernel(
    fields, density, thickness, col_hbm, row_hbm, coarse_out, flux_out, tend_out,
    g_in, col_in, row_in, col, row, g_high, g_low, send, recv, acc, part_in, osend, orecv, wsend, wrecv,
    load_sem, send_sem, recv_sem, part_sem, osend_sem, orecv_sem, wsend_sem, wrecv_sem,
):
    slab, lev = lax.axis_index("slab"), lax.axis_index("lev")
    core, chip = lax.rem(slab, 2), lax.div(slab, 2)
    z, y = lax.div(chip, 8), lax.rem(chip, 8)
    has_up, has_down = lev < 7, lev > 0

    load = pltpu.make_async_copy(fields.at[0], g_in, load_sem.at[0])
    load.start()
    col_load = pltpu.make_async_copy(col_hbm, col_in, load_sem.at[1])
    col_load.start()
    row_load = pltpu.make_async_copy(row_hbm.at[core], row_in, load_sem.at[2])
    row_load.start()

    barrier = pltpu.get_barrier_semaphore()

    def greet(s, carry):
        peer = lax.rem(chip + s, 32)
        pl.semaphore_signal(barrier, inc=1, device_id={"slab": 2 * peer + core})
        return carry

    lax.fori_loop(1, 32, greet, 0)
    pl.semaphore_signal(barrier, inc=1, device_id={"slab": 2 * chip + 1 - core})

    @pl.when(has_up)
    def _():
        pl.semaphore_signal(barrier, inc=1, device_id={"lev": lev + 1})

    @pl.when(has_down)
    def _():
        pl.semaphore_signal(barrier, inc=1, device_id={"lev": lev - 1})

    load.wait()
    for f in range(4):
        h, l = split(g_in[f])
        g_high[32 * f : 32 * f + 32] = h
        g_low[32 * f : 32 * f + 32] = l
    for f, (a, b) in enumerate(((0, 2), (1, 2), (3, 2), (0, 1))):
        h, l = split(g_in[a] * g_in[b])
        g_high[128 + 32 * f : 160 + 32 * f] = h
        g_low[128 + 32 * f : 160 + 32 * f] = l

    col_load.wait()
    h, l = split(col_in[...])
    col[:GRID, :128], col[:GRID, 128:] = h, l
    col[GRID:, :128], col[GRID:, 128:] = h[:1536], l[:1536]

    for n, k in enumerate(ORDER):
        zq = lax.rem(z + k, 4)
        turn = pl.ds(pl.multiple_of(512 * lax.rem(4 - zq, 4), 512), GRID)
        both = dot(g_high[...], col[turn])
        extra = dot(g_low[...], col[turn, :128])
        send[n] = both[:, :128] + both[:, 128:] + extra
        if n == 0:
            pl.semaphore_wait(barrier, 32 + has_up.astype(jnp.int32) + has_down.astype(jnp.int32))

        def push(s, carry, n=n, zq=zq):
            yq = lax.rem(y + s, 8)
            pltpu.make_async_remote_copy(
                src_ref=send.at[n, pl.ds(yq * 32, 32)],
                dst_ref=recv.at[z, pl.ds(y * 32, 32)],
                send_sem=send_sem.at[n],
                recv_sem=recv_sem.at[z],
                device_id={"slab": (zq * 8 + yq) * 2 + core},
            ).start()
            return carry

        lax.fori_loop(0 if k else 1, 8, push, 0)
        if k == 0:
            recv[z, pl.ds(y * 32, 32)] = send[n, pl.ds(y * 32, 32)]

    row_load.wait()
    h, l = split(row_in[...])
    row[0, :4], row[1, :4] = h, l
    row[0, 4:], row[1, 4:] = h[:3], l[:3]

    for n, k in enumerate(ORDER):
        zs = lax.rem(z + 4 - k, 4)
        size = 256 if k else 224
        pltpu.make_async_copy(recv.at[zs, pl.ds(0, size)], recv.at[zs, pl.ds(0, size)], recv_sem.at[zs]).wait()
        h, l = split(recv[zs])
        turn = pl.ds(lax.rem(4 - zs, 4), 4)
        both = dot(row[0, turn].reshape(512, 256), jnp.concatenate([h, l], axis=1))
        extra = dot(row[1, turn].reshape(512, 256), h)
        total = (both[:, :128] + both[:, 128:] + extra).reshape(4, 128, 128)
        if n:
            acc[...] += total
        else:
            acc[...] = total

    def cross(n):
        zq = lax.rem(z + ORDER[n], 4)
        return pltpu.make_async_remote_copy(
            src_ref=acc.at[zq, pl.ds(0, 64)],
            dst_ref=part_in.at[n],
            send_sem=part_sem.at[0, n],
            recv_sem=part_sem.at[1, n],
            device_id={"slab": 2 * chip + 1 - core},
        )

    for n in range(4):
        cross(n).start()

    for n, k in enumerate(ORDER):
        zq = lax.rem(z + k, 4)
        cross(n).wait_recv()
        osend[n] = acc[zq, 64:] + part_in[n]

        def give(s, carry, n=n, zq=zq):
            yq = lax.rem(y + s, 8)
            pltpu.make_async_remote_copy(
                src_ref=osend.at[n, pl.ds(yq * 8, 8)],
                dst_ref=orecv.at[z, pl.ds(y * 8, 8)],
                send_sem=osend_sem.at[n],
                recv_sem=orecv_sem.at[z],
                device_id={"slab": (zq * 8 + yq) * 2 + core},
            ).start()
            return carry

        lax.fori_loop(0 if k else 1, 8, give, 0)
        if k == 0:
            orecv[z, pl.ds(y * 8, 8)] = osend[n, pl.ds(y * 8, 8)]

    def lev_copy(n, side):
        return pltpu.make_async_remote_copy(
            src_ref=wsend.at[n],
            dst_ref=wrecv.at[side, n],
            send_sem=wsend_sem.at[side, n],
            recv_sem=wrecv_sem.at[side, n],
            device_id={"lev": lev + 1 if side == 0 else lev - 1},
        )

    for n, k in enumerate(ORDER):
        zs = lax.rem(z + 4 - k, 4)
        size = 64 if k else 56
        pltpu.make_async_copy(orecv.at[zs, pl.ds(0, size)], orecv.at[zs, pl.ds(0, size)], orecv_sem.at[zs]).wait()
        tile = [orecv[zs, 8 * f : 8 * f + 8] for f in range(8)]
        lanes = pl.ds(pl.multiple_of(zs * 128, 128), 128)
        for f in range(4):
            coarse_out[0, f, :, lanes] = tile[f]
        for f, (a, b) in enumerate(((0, 2), (1, 2), (3, 2), (0, 1))):
            flux = tile[4 + f] - tile[a] * tile[b]
            flux_out[0, f, :, lanes] = flux
            if f < 3:
                wsend[n, 8 * f : 8 * f + 8] = density[0] * flux

        @pl.when(has_up)
        def _(n=n):
            lev_copy(n, 0).start()

        @pl.when(has_down)
        def _(n=n):
            lev_copy(n, 1).start()

    @pl.when(jnp.logical_not(has_down))
    def _():
        wrecv[0] = jnp.zeros_like(wrecv[0])

    @pl.when(jnp.logical_not(has_up))
    def _():
        wrecv[1] = jnp.zeros_like(wrecv[1])

    factor = thickness[0] / (2.0 * density[0])
    for n, k in enumerate(ORDER):
        zs = lax.rem(z + 4 - k, 4)
        lanes = pl.ds(pl.multiple_of(zs * 128, 128), 128)

        @pl.when(has_down)
        def _(n=n):
            lev_copy(n, 0).wait_recv()

        @pl.when(has_up)
        def _(n=n):
            lev_copy(n, 1).wait_recv()

        for f in range(3):
            rows = slice(8 * f, 8 * f + 8)
            tend_out[0, f, :, lanes] = -(wrecv[1, n, rows] - wrecv[0, n, rows]) * factor

    for n, k in enumerate(ORDER):
        size = 256 if k else 224
        pltpu.make_async_copy(send.at[n, pl.ds(0, size)], send.at[n, pl.ds(0, size)], send_sem.at[n]).wait()
        size = 64 if k else 56
        pltpu.make_async_copy(osend.at[n, pl.ds(0, size)], osend.at[n, pl.ds(0, size)], osend_sem.at[n]).wait()
        cross(n).wait_send()

        @pl.when(has_up)
        def _(n=n):
            lev_copy(n, 0).wait_send()

        @pl.when(has_down)
        def _(n=n):
            lev_copy(n, 1).wait_send()


def shards(columns, rows, fields, density, thickness):
    anywhere = pl.BlockSpec(memory_space=pl.ANY)
    scalar = pl.BlockSpec(memory_space=pltpu.SMEM)
    vmem = pl.BlockSpec(memory_space=pltpu.VMEM)
    dma = pltpu.SemaphoreType.DMA
    return pl.pallas_call(
        kernel,
        out_shape=[jax.ShapeDtypeStruct((1, n, 8, TARGET), F32) for n in (4, 4, 3)],
        in_specs=[anywhere, scalar, scalar, anywhere, anywhere],
        out_specs=[vmem] * 3,
        scratch_shapes=[
            pltpu.VMEM((4, 32, GRID), F32),
            pltpu.VMEM((GRID, 128), F32),
            pltpu.VMEM((4, 128, 256), F32),
            pltpu.VMEM((GRID + 1536, 256), BF16),
            pltpu.VMEM((2, 7, 128, 256), BF16),
            pltpu.VMEM((256, GRID), BF16),
            pltpu.VMEM((256, GRID), BF16),
            pltpu.VMEM((4, 256, 128), F32),
            pltpu.VMEM((4, 256, 128), F32),
            pltpu.VMEM((4, 128, 128), F32),
            pltpu.VMEM((4, 64, 128), F32),
            pltpu.VMEM((4, 64, 128), F32),
            pltpu.VMEM((4, 64, 128), F32),
            pltpu.VMEM((4, 24, 128), F32),
            pltpu.VMEM((2, 4, 24, 128), F32),
            dma((3,)),
            dma((4,)),
            dma((4,)),
            dma((2, 4)),
            dma((4,)),
            dma((4,)),
            dma((2, 4)),
            dma((2, 4)),
        ],
        compiler_params=pltpu.CompilerParams(
            collective_id=0, has_side_effects=True, vmem_limit_bytes=40 * 1024 * 1024
        ),
    )(fields, density, thickness, columns, rows)


def solution(mesh):
    columns, rows = tables()
    placed = P("lev", None, "slab", None)
    return jax.shard_map(
        functools.partial(shards, columns, rows),
        mesh=mesh,
        in_specs=(placed, P("lev"), P("lev")),
        out_specs=(placed, placed, placed),
        check_vma=False,
    )
```

```python
import functools

import jax
import jax.numpy as jnp
import ml_dtypes
import numpy as np
from jax import lax
from jax.experimental import pallas as pl
from jax.experimental.pallas import tpu as pltpu
from jax.sharding import PartitionSpec as P

GRID = 2048
TARGET = 512
ORDER = (2, 1, 3, 0)
AROUND = (0, 4, 1, 5, 2, 6, 3, 7)
NEAREST = ((0, 1, 2, 3), (1, 0, 2, 3), (2, 3, 1, 0), (3, 2, 1, 0))
F32 = jnp.float32
BF16 = jnp.bfloat16


def tables():
    k = np.arange(1, TARGET // 2, dtype=np.float64)
    offsets = np.arange(GRID, dtype=np.float64)
    profile = (1.0 + 2.0 * np.cos(2.0 * np.pi * np.outer(offsets, k) / GRID).sum(1)) / GRID
    index = (GRID // TARGET * np.arange(TARGET)[:, None] - np.arange(GRID)[None, :]) % GRID
    matrix = profile[index].astype(np.float32)
    columns = np.ascontiguousarray(matrix[:128].T)
    first = matrix[:, :512].reshape(4, 8, 2, 8, 8, 2, 32)
    rows = [
        np.stack([first[:, :, c, :, :, core] for c in (1 - core, core)], axis=1).reshape(4, 128, 256)
        for core in range(2)
    ]
    return columns, np.stack(rows)


def split(value):
    high = value.astype(BF16)
    return high, (value - high.astype(F32)).astype(BF16)


def dot(a, b):
    return jnp.dot(a, b, preferred_element_type=F32)


def kernel(
    fields, density_hbm, thickness_hbm, col_hbm, row_hbm, out,
    density, thickness, g_in, col_in, row_in, col, row, g_high, g_low, send, recv, acc, part_in, osend, orecv, wsend, wrecv,
    load_sem, send_sem, recv_sem, part_sem, osend_sem, orecv_sem, wsend_sem, wrecv_sem,
):
    slab, lev = lax.axis_index("slab"), lax.axis_index("lev")
    core, chip = lax.rem(slab, 2), lax.div(slab, 2)
    z, y = lax.div(chip, 8), lax.rem(chip, 8)
    has_up, has_down = lev < 7, lev > 0
    near = [jnp.where(z < 2, jnp.where(z == 0, a, b), jnp.where(z == 2, c, d)) for a, b, c, d in zip(*NEAREST)]

    load = pltpu.make_async_copy(fields.at[0], g_in, load_sem.at[0])
    load.start()
    col_load = pltpu.make_async_copy(col_hbm, col_in, load_sem.at[1])
    col_load.start()
    row_load = pltpu.make_async_copy(row_hbm.at[core], row_in, load_sem.at[2])
    row_load.start()
    scalars = [
        pltpu.make_async_copy(density_hbm, density, load_sem.at[3]),
        pltpu.make_async_copy(thickness_hbm, thickness, load_sem.at[4]),
    ]
    for c in scalars:
        c.start()

    barrier = pltpu.get_barrier_semaphore()

    def greet(s, carry):
        peer = lax.rem(chip + s, 32)
        pl.semaphore_signal(barrier, inc=1, device_id={"slab": 2 * peer + core})
        return carry

    lax.fori_loop(1, 32, greet, 0)
    pl.semaphore_signal(barrier, inc=1, device_id={"slab": 2 * chip + 1 - core})

    @pl.when(has_up)
    def _():
        pl.semaphore_signal(barrier, inc=1, device_id={"lev": lev + 1})

    @pl.when(has_down)
    def _():
        pl.semaphore_signal(barrier, inc=1, device_id={"lev": lev - 1})

    load.wait()
    for f in range(4):
        h, l = split(g_in[f])
        g_high[32 * f : 32 * f + 32] = h
        g_low[32 * f : 32 * f + 32] = l
    for f, (a, b) in enumerate(((0, 2), (1, 2), (3, 2), (0, 1))):
        h, l = split(g_in[a] * g_in[b])
        g_high[128 + 32 * f : 160 + 32 * f] = h
        g_low[128 + 32 * f : 160 + 32 * f] = l

    col_load.wait()
    h, l = split(col_in[...])
    col[:GRID, :128], col[:GRID, 128:] = h, l
    col[GRID:, :128], col[GRID:, 128:] = h[:1536], l[:1536]

    for n, k in enumerate(ORDER):
        zq = lax.rem(z + k, 4)
        turn = pl.ds(pl.multiple_of(512 * lax.rem(4 - zq, 4), 512), GRID)
        both = dot(g_high[...], col[turn])
        extra = dot(g_low[...], col[turn, :128])
        send[n] = both[:, :128] + both[:, 128:] + extra
        if n == 0:
            pl.semaphore_wait(barrier, 32 + has_up.astype(jnp.int32) + has_down.astype(jnp.int32))

        for step in AROUND[0 if k else 1 :]:
            yq = lax.rem(y + step, 8)
            pltpu.make_async_remote_copy(
                src_ref=send.at[n, pl.ds(yq * 32, 32)],
                dst_ref=recv.at[z, pl.ds(y * 32, 32)],
                send_sem=send_sem.at[n],
                recv_sem=recv_sem.at[z],
                device_id={"slab": (zq * 8 + yq) * 2 + core},
            ).start()
        if k == 0:
            recv[z, pl.ds(y * 32, 32)] = send[n, pl.ds(y * 32, 32)]

    row_load.wait()
    for c in scalars:
        c.wait()
    h, l = split(row_in[...])
    row[0, :4], row[1, :4] = h, l
    row[0, 4:], row[1, 4:] = h[:3], l[:3]

    def cross(i):
        return pltpu.make_async_remote_copy(
            src_ref=acc.at[0, near[i]],
            dst_ref=part_in.at[i],
            send_sem=part_sem.at[0, i],
            recv_sem=part_sem.at[1, i],
            device_id={"slab": 2 * chip + 1 - core},
        )

    for n, k in enumerate(ORDER):
        zs = lax.rem(z + 4 - k, 4)
        size = 256 if k else 224
        pltpu.make_async_copy(recv.at[zs, pl.ds(0, size)], recv.at[zs, pl.ds(0, size)], recv_sem.at[zs]).wait()
        h, l = split(recv[zs])
        turn = pl.ds(lax.rem(4 - zs, 4), 4)
        pair = jnp.concatenate([h, l], axis=1)
        for half in range(2):
            part = slice(64 * half, 64 * half + 64)
            both = dot(row[0, turn, part].reshape(256, 256), pair)
            extra = dot(row[1, turn, part].reshape(256, 256), h)
            total = (both[:, :128] + both[:, 128:] + extra).reshape(4, 64, 128)
            if n:
                acc[half] += total
            else:
                acc[half] = total
            if n == 3 and half == 0:
                for i in reversed(range(4)):
                    cross(i).start()

    for i in reversed(range(4)):
        zq = near[i]
        cross(i).wait_recv()
        osend[i] = acc[1, zq] + part_in[i]
        for step in AROUND[0 if i else 1 :]:
            yq = lax.rem(y + step, 8)
            pltpu.make_async_remote_copy(
                src_ref=osend.at[i, pl.ds(yq * 8, 8)],
                dst_ref=orecv.at[z, pl.ds(y * 8, 8)],
                send_sem=osend_sem.at[i],
                recv_sem=orecv_sem.at[z],
                device_id={"slab": (zq * 8 + yq) * 2 + core},
            ).start()
        if i == 0:
            orecv[z, pl.ds(y * 8, 8)] = osend[i, pl.ds(y * 8, 8)]

    def lev_copy(n, side):
        return pltpu.make_async_remote_copy(
            src_ref=wsend.at[n],
            dst_ref=wrecv.at[side, n],
            send_sem=wsend_sem.at[side, n],
            recv_sem=wrecv_sem.at[side, n],
            device_id={"lev": lev + 1 if side == 0 else lev - 1},
        )

    for n in range(4):
        zs = near[n]
        size = 64 if n else 56
        pltpu.make_async_copy(orecv.at[zs, pl.ds(0, size)], orecv.at[zs, pl.ds(0, size)], orecv_sem.at[zs]).wait()
        tile = [orecv[zs, 8 * f : 8 * f + 8] for f in range(8)]
        lanes = pl.ds(pl.multiple_of(zs * 128, 128), 128)
        for f in range(4):
            out[f, :, lanes] = tile[f]
        for f, (a, b) in enumerate(((0, 2), (1, 2), (3, 2), (0, 1))):
            flux = tile[4 + f] - tile[a] * tile[b]
            out[4 + f, :, lanes] = flux
            if f < 3:
                wsend[n, 8 * f : 8 * f + 8] = density[0] * flux

        @pl.when(has_up)
        def _(n=n):
            lev_copy(n, 0).start()

        @pl.when(has_down)
        def _(n=n):
            lev_copy(n, 1).start()

    @pl.when(jnp.logical_not(has_down))
    def _():
        wrecv[0] = jnp.zeros_like(wrecv[0])

    @pl.when(jnp.logical_not(has_up))
    def _():
        wrecv[1] = jnp.zeros_like(wrecv[1])

    factor = thickness[0] / (2.0 * density[0])
    for n in range(4):
        zs = near[n]
        lanes = pl.ds(pl.multiple_of(zs * 128, 128), 128)

        @pl.when(has_down)
        def _(n=n):
            lev_copy(n, 0).wait_recv()

        @pl.when(has_up)
        def _(n=n):
            lev_copy(n, 1).wait_recv()

        for f in range(3):
            rows = slice(8 * f, 8 * f + 8)
            out[8 + f, :, lanes] = -(wrecv[1, n, rows] - wrecv[0, n, rows]) * factor

    for n, k in enumerate(ORDER):
        size = 256 if k else 224
        pltpu.make_async_copy(send.at[n, pl.ds(0, size)], send.at[n, pl.ds(0, size)], send_sem.at[n]).wait()
        size = 64 if n else 56
        pltpu.make_async_copy(osend.at[n, pl.ds(0, size)], osend.at[n, pl.ds(0, size)], osend_sem.at[n]).wait()
        cross(n).wait_send()

        @pl.when(has_up)
        def _(n=n):
            lev_copy(n, 0).wait_send()

        @pl.when(has_down)
        def _(n=n):
            lev_copy(n, 1).wait_send()


def shards(columns, rows, fields, density, thickness):
    hbm = pl.BlockSpec(memory_space=pltpu.HBM)
    vmem = pl.BlockSpec(memory_space=pltpu.VMEM)
    dma = pltpu.SemaphoreType.DMA
    out = pl.pallas_call(
        kernel,
        out_shape=jax.ShapeDtypeStruct((11, 8, TARGET), F32),
        in_specs=[hbm] * 5,
        out_specs=vmem,
        scratch_shapes=[
            pltpu.SMEM((1,), F32),
            pltpu.SMEM((1,), F32),
            pltpu.VMEM((4, 32, GRID), F32),
            pltpu.VMEM((GRID, 128), F32),
            pltpu.VMEM((4, 128, 256), F32),
            pltpu.VMEM((GRID + 1536, 256), BF16),
            pltpu.VMEM((2, 7, 128, 256), BF16),
            pltpu.VMEM((256, GRID), BF16),
            pltpu.VMEM((256, GRID), BF16),
            pltpu.VMEM((4, 256, 128), F32),
            pltpu.VMEM((4, 256, 128), F32),
            pltpu.VMEM((2, 4, 64, 128), F32),
            pltpu.VMEM((4, 64, 128), F32),
            pltpu.VMEM((4, 64, 128), F32),
            pltpu.VMEM((4, 64, 128), F32),
            pltpu.VMEM((4, 24, 128), F32),
            pltpu.VMEM((2, 4, 24, 128), F32),
            dma((5,)),
            dma((4,)),
            dma((4,)),
            dma((2, 4)),
            dma((4,)),
            dma((4,)),
            dma((2, 4)),
            dma((2, 4)),
        ],
        compiler_params=pltpu.CompilerParams(
            collective_id=0, has_side_effects=True, vmem_limit_bytes=54528 * 1024
        ),
    )(fields, density, thickness, columns, rows)
    return out[None, :4], out[None, 4:8], out[None, 8:]


def solution(mesh):
    columns, rows = tables()
    placed = P("lev", None, "slab", None)
    return jax.shard_map(
        functools.partial(shards, columns, rows),
        mesh=mesh,
        in_specs=(placed, P("lev"), P("lev")),
        out_specs=(placed, placed, placed),
        check_vma=False,
    )
```

```python
import functools

import jax
import jax.numpy as jnp
import ml_dtypes
import numpy as np
from jax import lax
from jax.experimental import pallas as pl
from jax.experimental.pallas import tpu as pltpu
from jax.sharding import PartitionSpec as P

GRID = 2048
TARGET = 512
SENT = 25
ORDER = (2, 1, 3, 0)
PRODUCTS = ((0, 2), (1, 2), (3, 2), (0, 1))
AROUND = (0, 4, 1, 5, 2, 6, 3, 7)
NEAREST = ((0, 1, 2, 3), (1, 0, 2, 3), (2, 3, 1, 0), (3, 2, 1, 0))
F32 = jnp.float32
BF16 = jnp.bfloat16


def tables():
    k = np.arange(1, TARGET // 2, dtype=np.float64)
    offsets = np.arange(GRID, dtype=np.float64)
    profile = (1.0 + 2.0 * np.cos(2.0 * np.pi * np.outer(offsets, k) / GRID).sum(1)) / GRID
    index = (GRID // TARGET * np.arange(TARGET)[:, None] - np.arange(GRID)[None, :]) % GRID
    matrix = profile[index].astype(np.float32)
    columns = np.ascontiguousarray(matrix[:128].T)
    first = matrix[:, :512].reshape(4, 8, 2, 8, 8, 2, 8, 4)[..., 1:].swapaxes(6, 7)
    rows = [
        np.stack([first[:, :, c, :, :, core] for c in (1 - core, core)], axis=1).reshape(4, 128, 192)
        for core in range(2)
    ]
    return columns, np.stack(rows)


def split(value):
    high = value.astype(BF16)
    return high, (value - high.astype(F32)).astype(BF16)


def dot(a, b):
    return jnp.dot(a, b, preferred_element_type=F32)


def kernel(
    fields, density_hbm, thickness_hbm, col_hbm, row_hbm, out,
    density, thickness, g_in, col_in, row_in, col, row, g_high, g_low, whole, send, recv, local, acc, part_in, osend, orecv, wsend, wrecv,
    load_sem, send_sem, recv_sem, part_sem, osend_sem, orecv_sem, wsend_sem, wrecv_sem,
):
    slab, lev = lax.axis_index("slab"), lax.axis_index("lev")
    core, chip = lax.rem(slab, 2), lax.div(slab, 2)
    z, y = lax.div(chip, 8), lax.rem(chip, 8)
    has_up, has_down = lev < 7, lev > 0
    near = [jnp.where(z < 2, jnp.where(z == 0, a, b), jnp.where(z == 2, c, d)) for a, b, c, d in zip(*NEAREST)]

    load = pltpu.make_async_copy(fields.at[0], g_in, load_sem.at[0])
    load.start()
    col_load = pltpu.make_async_copy(col_hbm, col_in, load_sem.at[1])
    col_load.start()
    row_load = pltpu.make_async_copy(row_hbm.at[core], row_in, load_sem.at[2])
    row_load.start()
    scalars = [
        pltpu.make_async_copy(density_hbm, density, load_sem.at[3]),
        pltpu.make_async_copy(thickness_hbm, thickness, load_sem.at[4]),
    ]
    for c in scalars:
        c.start()

    barrier = pltpu.get_barrier_semaphore()

    for i in reversed(range(4)):
        for step in AROUND[0 if i else 1 :]:
            peer = near[i] * 8 + lax.rem(y + step, 8)
            pl.semaphore_signal(barrier, inc=1, device_id={"slab": 2 * peer + core})
    pl.semaphore_signal(barrier, inc=1, device_id={"slab": 2 * chip + 1 - core})

    @pl.when(has_up)
    def _():
        pl.semaphore_signal(barrier, inc=1, device_id={"lev": lev + 1})

    @pl.when(has_down)
    def _():
        pl.semaphore_signal(barrier, inc=1, device_id={"lev": lev - 1})

    load.wait()
    fine = [g_in[f] for f in range(4)]
    fine += [fine[a] * fine[b] for a, b in PRODUCTS]
    for f in range(8):
        h, l = split(fine[f])
        g_high[32 * f : 32 * f + 32] = h
        g_low[32 * f : 32 * f + 32] = l

    col_load.wait()
    h, l = split(col_in[...])
    col[:GRID, :128], col[:GRID, 128:] = h, l
    col[GRID:, :128], col[GRID:, 128:] = h[:1536], l[:1536]

    alternating = 1.0 - 2.0 * lax.rem(lax.broadcasted_iota(jnp.int32, (8, 128), 0), 2).astype(F32)
    for n, k in enumerate(ORDER):
        zq = lax.rem(z + k, 4)
        turn = pl.ds(pl.multiple_of(512 * lax.rem(4 - zq, 4), 512), GRID)
        both = dot(g_high[...], col[turn])
        extra = dot(g_low[...], col[turn, :128])
        whole[...] = both[:, :128] + both[:, 128:] + extra
        for f in range(8):
            for s in (1, 2, 3):
                send[n, f, 8 * s - 8 : 8 * s] = whole[pl.ds(32 * f + s, 8, 4)]
            kept = whole[pl.ds(32 * f, 8, 4)]
            send[n, f, 24:25] = jnp.sum(kept * alternating, axis=0, keepdims=True)
            local[zq, f] = 0.25 * kept
        if n == 0:
            pl.semaphore_wait(barrier, 32 + has_up.astype(jnp.int32) + has_down.astype(jnp.int32))

        for step in AROUND[0 if k else 1 :]:
            yq = lax.rem(y + step, 8)
            pltpu.make_async_remote_copy(
                src_ref=send.at[n, yq, pl.ds(0, SENT)],
                dst_ref=recv.at[z, y, pl.ds(0, SENT)],
                send_sem=send_sem.at[n],
                recv_sem=recv_sem.at[z],
                device_id={"slab": (zq * 8 + yq) * 2 + core},
            ).start()
        if k == 0:
            recv[z, y] = send[n, y]

    row_load.wait()
    for c in scalars:
        c.wait()
    h, l = split(row_in[...])
    row[0, :4], row[1, :4] = h, l
    row[0, 4:], row[1, 4:] = h[:3], l[:3]

    def cross(i):
        return pltpu.make_async_remote_copy(
            src_ref=acc.at[0, near[i]],
            dst_ref=part_in.at[i],
            send_sem=part_sem.at[0, i],
            recv_sem=part_sem.at[1, i],
            device_id={"slab": 2 * chip + 1 - core},
        )

    for n, k in enumerate(ORDER):
        zs = lax.rem(z + 4 - k, 4)
        arrived = recv.at[zs, pl.ds(0, 8 if k else 7), pl.ds(0, SENT)]
        pltpu.make_async_copy(arrived, arrived, recv_sem.at[zs]).wait()
        h, l = split(recv[zs, :, :24].reshape(192, 128))
        removed = jnp.sum(recv[zs, :, 24], axis=0, keepdims=True) * alternating * (1.0 / GRID)
        turn = pl.ds(lax.rem(4 - zs, 4), 4)
        pair = jnp.concatenate([h, l], axis=1)
        for half in range(2):
            part = slice(64 * half, 64 * half + 64)
            both = dot(row[0, turn, part].reshape(256, 192), pair)
            extra = dot(row[1, turn, part].reshape(256, 192), h)
            total = (both[:, :128] + both[:, 128:] + extra).reshape(4, 8, 8, 128)
            total = (total - removed).reshape(4, 64, 128)
            if n:
                acc[half] += total
            else:
                acc[half] = total
            if n == 3 and half == 0:
                for i in reversed(range(4)):
                    cross(i).start()

    for i in reversed(range(4)):
        zq = near[i]
        cross(i).wait_recv()
        osend[i] = acc[1, zq] + part_in[i]
        for step in AROUND[0 if i else 1 :]:
            yq = lax.rem(y + step, 8)
            pltpu.make_async_remote_copy(
                src_ref=osend.at[i, pl.ds(yq * 8, 8)],
                dst_ref=orecv.at[z, pl.ds(y * 8, 8)],
                send_sem=osend_sem.at[i],
                recv_sem=orecv_sem.at[z],
                device_id={"slab": (zq * 8 + yq) * 2 + core},
            ).start()
        if i == 0:
            orecv[z, pl.ds(y * 8, 8)] = osend[i, pl.ds(y * 8, 8)]

    def lev_copy(n, side):
        return pltpu.make_async_remote_copy(
            src_ref=wsend.at[n],
            dst_ref=wrecv.at[side, n],
            send_sem=wsend_sem.at[side, n],
            recv_sem=wrecv_sem.at[side, n],
            device_id={"lev": lev + 1 if side == 0 else lev - 1},
        )

    for n in range(4):
        zs = near[n]
        size = 64 if n else 56
        pltpu.make_async_copy(orecv.at[zs, pl.ds(0, size)], orecv.at[zs, pl.ds(0, size)], orecv_sem.at[zs]).wait()
        tile = [orecv[zs, 8 * f : 8 * f + 8] + local[zs, f] for f in range(8)]
        lanes = pl.ds(pl.multiple_of(zs * 128, 128), 128)
        for f in range(4):
            out[f, :, lanes] = tile[f]
        for f, (a, b) in enumerate(PRODUCTS):
            flux = tile[4 + f] - tile[a] * tile[b]
            out[4 + f, :, lanes] = flux
            if f < 3:
                wsend[n, 8 * f : 8 * f + 8] = density[0] * flux

        @pl.when(has_up)
        def _(n=n):
            lev_copy(n, 0).start()

        @pl.when(has_down)
        def _(n=n):
            lev_copy(n, 1).start()

    @pl.when(jnp.logical_not(has_down))
    def _():
        wrecv[0] = jnp.zeros_like(wrecv[0])

    @pl.when(jnp.logical_not(has_up))
    def _():
        wrecv[1] = jnp.zeros_like(wrecv[1])

    factor = thickness[0] / (2.0 * density[0])
    for n in range(4):
        zs = near[n]
        lanes = pl.ds(pl.multiple_of(zs * 128, 128), 128)

        @pl.when(has_down)
        def _(n=n):
            lev_copy(n, 0).wait_recv()

        @pl.when(has_up)
        def _(n=n):
            lev_copy(n, 1).wait_recv()

        for f in range(3):
            rows = slice(8 * f, 8 * f + 8)
            out[8 + f, :, lanes] = -(wrecv[1, n, rows] - wrecv[0, n, rows]) * factor

    for n, k in enumerate(ORDER):
        sent = send.at[n, pl.ds(0, 8 if k else 7), pl.ds(0, SENT)]
        pltpu.make_async_copy(sent, sent, send_sem.at[n]).wait()
        size = 64 if n else 56
        pltpu.make_async_copy(osend.at[n, pl.ds(0, size)], osend.at[n, pl.ds(0, size)], osend_sem.at[n]).wait()
        cross(n).wait_send()

        @pl.when(has_up)
        def _(n=n):
            lev_copy(n, 0).wait_send()

        @pl.when(has_down)
        def _(n=n):
            lev_copy(n, 1).wait_send()


def shards(columns, rows, fields, density, thickness):
    hbm = pl.BlockSpec(memory_space=pltpu.HBM)
    vmem = pl.BlockSpec(memory_space=pltpu.VMEM)
    dma = pltpu.SemaphoreType.DMA
    out = pl.pallas_call(
        kernel,
        out_shape=jax.ShapeDtypeStruct((11, 8, TARGET), F32),
        in_specs=[hbm] * 5,
        out_specs=vmem,
        scratch_shapes=[
            pltpu.SMEM((1,), F32),
            pltpu.SMEM((1,), F32),
            pltpu.VMEM((4, 32, GRID), F32),
            pltpu.VMEM((GRID, 128), F32),
            pltpu.VMEM((4, 128, 192), F32),
            pltpu.VMEM((GRID + 1536, 256), BF16),
            pltpu.VMEM((2, 7, 128, 192), BF16),
            pltpu.VMEM((256, GRID), BF16),
            pltpu.VMEM((256, GRID), BF16),
            pltpu.VMEM((256, 128), F32),
            pltpu.VMEM((4, 8, 32, 128), F32),
            pltpu.VMEM((4, 8, 32, 128), F32),
            pltpu.VMEM((4, 8, 8, 128), F32),
            pltpu.VMEM((2, 4, 64, 128), F32),
            pltpu.VMEM((4, 64, 128), F32),
            pltpu.VMEM((4, 64, 128), F32),
            pltpu.VMEM((4, 64, 128), F32),
            pltpu.VMEM((4, 24, 128), F32),
            pltpu.VMEM((2, 4, 24, 128), F32),
            dma((5,)),
            dma((4,)),
            dma((4,)),
            dma((2, 4)),
            dma((4,)),
            dma((4,)),
            dma((2, 4)),
            dma((2, 4)),
        ],
        compiler_params=pltpu.CompilerParams(
            collective_id=0, has_side_effects=True, vmem_limit_bytes=54528 * 1024
        ),
    )(fields, density, thickness, columns, rows)
    return out[None, :4], out[None, 4:8], out[None, 8:]


def solution(mesh):
    columns, rows = tables()
    placed = P("lev", None, "slab", None)
    return jax.shard_map(
        functools.partial(shards, columns, rows),
        mesh=mesh,
        in_specs=(placed, P("lev"), P("lev")),
        out_specs=(placed, placed, placed),
        check_vma=False,
    )
```

```python
import functools

import jax
import jax.numpy as jnp
import ml_dtypes
import numpy as np
from jax import lax
from jax.experimental import pallas as pl
from jax.experimental.pallas import tpu as pltpu
from jax.sharding import PartitionSpec as P

GRID = 2048
TARGET = 512
SENT = 25
ORDER = (2, 1, 3, 0)
PRODUCTS = ((0, 2), (1, 2), (3, 2), (0, 1))
AROUND = (0, 4, 1, 5, 2, 6, 3, 7)
NEAREST = ((0, 1, 2, 3), (1, 0, 2, 3), (2, 3, 1, 0), (3, 2, 1, 0))
F32 = jnp.float32
BF16 = jnp.bfloat16


def tables():
    k = np.arange(1, TARGET // 2, dtype=np.float64)
    offsets = np.arange(GRID, dtype=np.float64)
    profile = (1.0 + 2.0 * np.cos(2.0 * np.pi * np.outer(offsets, k) / GRID).sum(1)) / GRID
    index = (GRID // TARGET * np.arange(TARGET)[:, None] - np.arange(GRID)[None, :]) % GRID
    matrix = profile[index].astype(np.float32)
    columns = np.ascontiguousarray(matrix[:128].T)
    first = matrix[:, :512].reshape(4, 8, 2, 8, 8, 2, 8, 4)[..., 1:].swapaxes(6, 7)
    rows = [
        np.stack([first[:, :, c, :, :, core] for c in (1 - core, core)], axis=1).reshape(4, 128, 192)
        for core in range(2)
    ]
    return columns, np.stack(rows)


def split(value):
    high = value.astype(BF16)
    return high, (value - high.astype(F32)).astype(BF16)


def dot(a, b):
    return jnp.dot(a, b, preferred_element_type=F32)


def kernel(
    fields, density_hbm, thickness_hbm, col_hbm, row_hbm, out,
    density, thickness, g_in, col_in, row_in, col, row, g_high, g_low, whole, send, recv, local, acc, part_in, osend, orecv, wsend, wrecv,
    load_sem, send_sem, recv_sem, part_sem, osend_sem, orecv_sem, wsend_sem, wrecv_sem, level_sem,
):
    slab, lev = lax.axis_index("slab"), lax.axis_index("lev")
    core, chip = lax.rem(slab, 2), lax.div(slab, 2)
    z, y = lax.div(chip, 8), lax.rem(chip, 8)
    has_up, has_down = lev < 7, lev > 0
    even = lax.rem(lev, 2) == 0
    neighbours = has_up.astype(jnp.int32) + has_down.astype(jnp.int32)
    near = [jnp.where(z < 2, jnp.where(z == 0, a, b), jnp.where(z == 2, c, d)) for a, b, c, d in zip(*NEAREST)]

    barrier = pltpu.get_barrier_semaphore()

    for i in reversed(range(4)):
        for step in AROUND[0 if i else 1 :]:
            peer = near[i] * 8 + lax.rem(y + step, 8)
            pl.semaphore_signal(barrier, inc=1, device_id={"slab": 2 * peer + core})
    pl.semaphore_signal(barrier, inc=1, device_id={"slab": 2 * chip + 1 - core})

    def greet_levels(semaphore):
        @pl.when(has_up)
        def _():
            pl.semaphore_signal(semaphore, inc=1, device_id={"lev": lev + 1})

        @pl.when(has_down)
        def _():
            pl.semaphore_signal(semaphore, inc=1, device_id={"lev": lev - 1})

    @pl.when(even)
    def _():
        greet_levels(barrier)

    load = pltpu.make_async_copy(fields.at[0], g_in, load_sem.at[0])
    load.start()
    col_load = pltpu.make_async_copy(col_hbm, col_in, load_sem.at[1])
    col_load.start()
    row_load = pltpu.make_async_copy(row_hbm.at[core], row_in, load_sem.at[2])
    row_load.start()
    scalars = [
        pltpu.make_async_copy(density_hbm, density, load_sem.at[3]),
        pltpu.make_async_copy(thickness_hbm, thickness, load_sem.at[4]),
    ]
    for c in scalars:
        c.start()

    load.wait()
    fine = [g_in[f] for f in range(4)]
    fine += [fine[a] * fine[b] for a, b in PRODUCTS]
    for f in range(8):
        h, l = split(fine[f])
        g_high[32 * f : 32 * f + 32] = h
        g_low[32 * f : 32 * f + 32] = l

    col_load.wait()
    h, l = split(col_in[...])
    col[:GRID, :128], col[:GRID, 128:] = h, l
    col[GRID:, :128], col[GRID:, 128:] = h[:1536], l[:1536]

    alternating = 1.0 - 2.0 * lax.rem(lax.broadcasted_iota(jnp.int32, (8, 128), 0), 2).astype(F32)
    for n, k in enumerate(ORDER):
        zq = lax.rem(z + k, 4)
        turn = pl.ds(pl.multiple_of(512 * lax.rem(4 - zq, 4), 512), GRID)
        both = dot(g_high[...], col[turn])
        extra = dot(g_low[...], col[turn, :128])
        whole[...] = both[:, :128] + both[:, 128:] + extra
        for f in range(8):
            for s in (1, 2, 3):
                send[n, f, 8 * s - 8 : 8 * s] = whole[pl.ds(32 * f + s, 8, 4)]
            kept = whole[pl.ds(32 * f, 8, 4)]
            send[n, f, 24:25] = jnp.sum(kept * alternating, axis=0, keepdims=True)
            local[zq, f] = 0.25 * kept
        if n == 0:
            pl.semaphore_wait(barrier, 32 + jnp.where(even, 0, neighbours))

            @pl.when(jnp.logical_not(even))
            def _():
                greet_levels(level_sem)


        for step in AROUND[0 if k else 1 :]:
            yq = lax.rem(y + step, 8)
            pltpu.make_async_remote_copy(
                src_ref=send.at[n, yq, pl.ds(0, SENT)],
                dst_ref=recv.at[z, y, pl.ds(0, SENT)],
                send_sem=send_sem.at[n],
                recv_sem=recv_sem.at[z],
                device_id={"slab": (zq * 8 + yq) * 2 + core},
            ).start()
        if k == 0:
            recv[z, y] = send[n, y]

    row_load.wait()
    for c in scalars:
        c.wait()
    h, l = split(row_in[...])
    row[0, :4], row[1, :4] = h, l
    row[0, 4:], row[1, 4:] = h[:3], l[:3]

    def cross(i):
        return pltpu.make_async_remote_copy(
            src_ref=acc.at[0, near[i]],
            dst_ref=part_in.at[i],
            send_sem=part_sem.at[0, i],
            recv_sem=part_sem.at[1, i],
            device_id={"slab": 2 * chip + 1 - core},
        )

    for n, k in enumerate(ORDER):
        zs = lax.rem(z + 4 - k, 4)
        arrived = recv.at[zs, pl.ds(0, 8 if k else 7), pl.ds(0, SENT)]
        pltpu.make_async_copy(arrived, arrived, recv_sem.at[zs]).wait()
        h, l = split(recv[zs, :, :24].reshape(192, 128))
        removed = jnp.sum(recv[zs, :, 24], axis=0, keepdims=True) * alternating * (1.0 / GRID)
        turn = pl.ds(lax.rem(4 - zs, 4), 4)
        pair = jnp.concatenate([h, l], axis=1)
        for half in range(2):
            part = slice(64 * half, 64 * half + 64)
            both = dot(row[0, turn, part].reshape(256, 192), pair)
            extra = dot(row[1, turn, part].reshape(256, 192), h)
            total = (both[:, :128] + both[:, 128:] + extra).reshape(4, 8, 8, 128)
            total = (total - removed).reshape(4, 64, 128)
            if n:
                acc[half] += total
            else:
                acc[half] = total
            if n == 3 and half == 0:
                for i in reversed(range(4)):
                    cross(i).start()

    for i in reversed(range(4)):
        zq = near[i]
        cross(i).wait_recv()
        osend[i] = acc[1, zq] + part_in[i]
        for step in AROUND[0 if i else 1 :]:
            yq = lax.rem(y + step, 8)
            pltpu.make_async_remote_copy(
                src_ref=osend.at[i, pl.ds(yq * 8, 8)],
                dst_ref=orecv.at[z, pl.ds(y * 8, 8)],
                send_sem=osend_sem.at[i],
                recv_sem=orecv_sem.at[z],
                device_id={"slab": (zq * 8 + yq) * 2 + core},
            ).start()
        if i == 0:
            orecv[z, pl.ds(y * 8, 8)] = osend[i, pl.ds(y * 8, 8)]

    def lev_copy(n, side):
        return pltpu.make_async_remote_copy(
            src_ref=wsend.at[n],
            dst_ref=wrecv.at[side, n],
            send_sem=wsend_sem.at[side, n],
            recv_sem=wrecv_sem.at[side, n],
            device_id={"lev": lev + 1 if side == 0 else lev - 1},
        )

    @pl.when(even)
    def _():
        pl.semaphore_wait(level_sem, neighbours)

    for n in range(4):
        zs = near[n]
        size = 64 if n else 56
        pltpu.make_async_copy(orecv.at[zs, pl.ds(0, size)], orecv.at[zs, pl.ds(0, size)], orecv_sem.at[zs]).wait()
        tile = [orecv[zs, 8 * f : 8 * f + 8] + local[zs, f] for f in range(8)]
        lanes = pl.ds(pl.multiple_of(zs * 128, 128), 128)
        for f in range(4):
            out[f, :, lanes] = tile[f]
        for f, (a, b) in enumerate(PRODUCTS):
            flux = tile[4 + f] - tile[a] * tile[b]
            out[4 + f, :, lanes] = flux
            if f < 3:
                wsend[n, 8 * f : 8 * f + 8] = density[0] * flux

        @pl.when(has_up)
        def _(n=n):
            lev_copy(n, 0).start()

        @pl.when(has_down)
        def _(n=n):
            lev_copy(n, 1).start()

    @pl.when(jnp.logical_not(has_down))
    def _():
        wrecv[0] = jnp.zeros_like(wrecv[0])

    @pl.when(jnp.logical_not(has_up))
    def _():
        wrecv[1] = jnp.zeros_like(wrecv[1])

    for n, k in enumerate(ORDER):
        sent = send.at[n, pl.ds(0, 8 if k else 7), pl.ds(0, SENT)]
        pltpu.make_async_copy(sent, sent, send_sem.at[n]).wait()
        size = 64 if n else 56
        pltpu.make_async_copy(osend.at[n, pl.ds(0, size)], osend.at[n, pl.ds(0, size)], osend_sem.at[n]).wait()
        cross(n).wait_send()

    @pl.when(has_down)
    def _():
        for n in range(4):
            lev_copy(n, 1).wait_send()
            lev_copy(n, 0).wait_recv()

    @pl.when(has_up)
    def _():
        for n in range(4):
            lev_copy(n, 0).wait_send()
            lev_copy(n, 1).wait_recv()

    factor = thickness[0] / (2.0 * density[0])
    for n in range(4):
        lanes = pl.ds(pl.multiple_of(near[n] * 128, 128), 128)
        for f in range(3):
            rows = slice(8 * f, 8 * f + 8)
            out[8 + f, :, lanes] = -(wrecv[1, n, rows] - wrecv[0, n, rows]) * factor


def shards(columns, rows, fields, density, thickness):
    hbm = pl.BlockSpec(memory_space=pltpu.HBM)
    vmem = pl.BlockSpec(memory_space=pltpu.VMEM)
    dma = pltpu.SemaphoreType.DMA
    out = pl.pallas_call(
        kernel,
        out_shape=jax.ShapeDtypeStruct((11, 8, TARGET), F32),
        in_specs=[hbm] * 5,
        out_specs=vmem,
        scratch_shapes=[
            pltpu.SMEM((1,), F32),
            pltpu.SMEM((1,), F32),
            pltpu.VMEM((4, 32, GRID), F32),
            pltpu.VMEM((GRID, 128), F32),
            pltpu.VMEM((4, 128, 192), F32),
            pltpu.VMEM((GRID + 1536, 256), BF16),
            pltpu.VMEM((2, 7, 128, 192), BF16),
            pltpu.VMEM((256, GRID), BF16),
            pltpu.VMEM((256, GRID), BF16),
            pltpu.VMEM((256, 128), F32),
            pltpu.VMEM((4, 8, 32, 128), F32),
            pltpu.VMEM((4, 8, 32, 128), F32),
            pltpu.VMEM((4, 8, 8, 128), F32),
            pltpu.VMEM((2, 4, 64, 128), F32),
            pltpu.VMEM((4, 64, 128), F32),
            pltpu.VMEM((4, 64, 128), F32),
            pltpu.VMEM((4, 64, 128), F32),
            pltpu.VMEM((4, 24, 128), F32),
            pltpu.VMEM((2, 4, 24, 128), F32),
            dma((5,)),
            dma((4,)),
            dma((4,)),
            dma((2, 4)),
            dma((4,)),
            dma((4,)),
            dma((2, 4)),
            dma((2, 4)),
            pltpu.SemaphoreType.REGULAR,
        ],
        compiler_params=pltpu.CompilerParams(
            collective_id=0, has_side_effects=True, vmem_limit_bytes=54528 * 1024
        ),
    )(fields, density, thickness, columns, rows)
    return out[None, :4], out[None, 4:8], out[None, 8:]


def solution(mesh):
    columns, rows = tables()
    placed = P("lev", None, "slab", None)
    return jax.shard_map(
        functools.partial(shards, columns, rows),
        mesh=mesh,
        in_specs=(placed, P("lev"), P("lev")),
        out_specs=(placed, placed, placed),
        check_vma=False,
    )
```

```python
import functools

import jax
import jax.numpy as jnp
import ml_dtypes
import numpy as np
from jax import lax
from jax.experimental import pallas as pl
from jax.experimental.pallas import tpu as pltpu
from jax.sharding import PartitionSpec as P

GRID = 2048
TARGET = 512
SENT = 25
ORDER = (2, 1, 3, 0)
PRODUCTS = ((0, 2), (1, 2), (3, 2), (0, 1))
AROUND = (0, 4, 1, 5, 2, 6, 3, 7)
NEAREST = ((0, 1, 2, 3), (1, 0, 2, 3), (2, 3, 1, 0), (3, 2, 1, 0))
F32 = jnp.float32
BF16 = jnp.bfloat16


def tables():
    k = np.arange(1, TARGET // 2, dtype=np.float64)
    offsets = np.arange(GRID, dtype=np.float64)
    profile = (1.0 + 2.0 * np.cos(2.0 * np.pi * np.outer(offsets, k) / GRID).sum(1)) / GRID
    index = (GRID // TARGET * np.arange(TARGET)[:, None] - np.arange(GRID)[None, :]) % GRID
    matrix = profile[index].astype(np.float32)
    columns = np.ascontiguousarray(matrix[:128].T)
    first = matrix[:, :512].reshape(4, 8, 2, 8, 8, 2, 8, 4)[..., 1:].swapaxes(6, 7)
    rows = [
        np.stack([first[:, :, c, :, :, core] for c in (1 - core, core)], axis=1).reshape(4, 128, 192)
        for core in range(2)
    ]
    return columns, np.stack(rows)


def split(value):
    high = value.astype(BF16)
    return high, (value - high.astype(F32)).astype(BF16)


def dot(a, b):
    return jnp.dot(a, b, preferred_element_type=F32)


def kernel(
    fields, density_hbm, thickness_hbm, col_hbm, row_hbm, out,
    density, thickness, g_in, col_in, row_in, col, row, g_high, g_low, whole, send, recv, local, acc, part_in, osend, orecv, wsend, wrecv,
    load_sem, send_sem, recv_sem, part_sem, osend_sem, orecv_sem, wsend_sem, wrecv_sem, level_sem,
):
    slab, lev = lax.axis_index("slab"), lax.axis_index("lev")
    core, chip = lax.rem(slab, 2), lax.div(slab, 2)
    z, y = lax.div(chip, 8), lax.rem(chip, 8)
    has_up, has_down = lev < 7, lev > 0
    even = lax.rem(lev, 2) == 0
    neighbours = has_up.astype(jnp.int32) + has_down.astype(jnp.int32)
    near = [jnp.where(z < 2, jnp.where(z == 0, a, b), jnp.where(z == 2, c, d)) for a, b, c, d in zip(*NEAREST)]

    barrier = pltpu.get_barrier_semaphore()

    for i in reversed(range(4)):
        for step in AROUND[0 if i else 1 :]:
            peer = near[i] * 8 + lax.rem(y + step, 8)
            pl.semaphore_signal(barrier, inc=1, device_id={"slab": 2 * peer + core})
    pl.semaphore_signal(barrier, inc=1, device_id={"slab": 2 * chip + 1 - core})

    def greet_levels(semaphore):
        @pl.when(has_up)
        def _():
            pl.semaphore_signal(semaphore, inc=1, device_id={"lev": lev + 1})

        @pl.when(has_down)
        def _():
            pl.semaphore_signal(semaphore, inc=1, device_id={"lev": lev - 1})

    @pl.when(even)
    def _():
        greet_levels(barrier)

    load = pltpu.make_async_copy(fields.at[0], g_in, load_sem.at[0])
    load.start()
    col_load = pltpu.make_async_copy(col_hbm, col_in, load_sem.at[1])
    col_load.start()
    row_load = pltpu.make_async_copy(row_hbm.at[core], row_in, load_sem.at[2])
    row_load.start()
    scalars = [
        pltpu.make_async_copy(density_hbm, density, load_sem.at[3]),
        pltpu.make_async_copy(thickness_hbm, thickness, load_sem.at[4]),
    ]
    for c in scalars:
        c.start()

    load.wait()
    fine = [g_in[f] for f in range(4)]
    fine += [fine[a] * fine[b] for a, b in PRODUCTS]
    for f in range(8):
        h, l = split(fine[f])
        g_high[32 * f : 32 * f + 32] = h
        g_low[32 * f : 32 * f + 32] = l

    col_load.wait()
    h, l = split(col_in[...])
    col[:GRID, :128], col[:GRID, 128:] = h, l
    col[GRID:, :128], col[GRID:, 128:] = h[:1536], l[:1536]

    alternating = 1.0 - 2.0 * lax.rem(lax.broadcasted_iota(jnp.int32, (8, 128), 0), 2).astype(F32)
    for n, k in enumerate(ORDER):
        zq = lax.rem(z + k, 4)
        turn = pl.ds(pl.multiple_of(512 * lax.rem(4 - zq, 4), 512), GRID)
        both = dot(g_high[...], col[turn])
        extra = dot(g_low[...], col[turn, :128])
        whole[...] = both[:, :128] + both[:, 128:] + extra
        for f in range(8):
            for s in (1, 2, 3):
                send[n, f, 8 * s - 8 : 8 * s] = whole[pl.ds(32 * f + s, 8, 4)]
            kept = whole[pl.ds(32 * f, 8, 4)]
            send[n, f, 24:25] = jnp.sum(kept * alternating, axis=0, keepdims=True)
            local[zq, f] = 0.25 * kept
        if n == 0:
            pl.semaphore_wait(barrier, 32 + jnp.where(even, 0, neighbours))

            @pl.when(jnp.logical_not(even))
            def _():
                greet_levels(level_sem)


        for step in AROUND[0 if k else 1 :]:
            yq = lax.rem(y + step, 8)
            pltpu.make_async_remote_copy(
                src_ref=send.at[n, yq, pl.ds(0, SENT)],
                dst_ref=recv.at[z, y, pl.ds(0, SENT)],
                send_sem=send_sem.at[n],
                recv_sem=recv_sem.at[z],
                device_id={"slab": (zq * 8 + yq) * 2 + core},
            ).start()
        if k == 0:
            recv[z, y] = send[n, y]

    row_load.wait()
    for c in scalars:
        c.wait()
    h, l = split(row_in[...])
    row[0, :4], row[1, :4] = h, l
    row[0, 4:], row[1, 4:] = h[:3], l[:3]

    def cross(i):
        return pltpu.make_async_remote_copy(
            src_ref=acc.at[0, near[i]],
            dst_ref=part_in.at[i],
            send_sem=part_sem.at[0, i],
            recv_sem=part_sem.at[1, i],
            device_id={"slab": 2 * chip + 1 - core},
        )

    for n, k in enumerate(ORDER):
        zs = lax.rem(z + 4 - k, 4)
        arrived = recv.at[zs, pl.ds(0, 8 if k else 7), pl.ds(0, SENT)]
        pltpu.make_async_copy(arrived, arrived, recv_sem.at[zs]).wait()
        h, l = split(recv[zs, :, :24].reshape(192, 128))
        removed = jnp.sum(recv[zs, :, 24], axis=0, keepdims=True) * alternating * (1.0 / GRID)
        turn = pl.ds(lax.rem(4 - zs, 4), 4)
        pair = jnp.concatenate([h, l], axis=1)
        for half in range(2):
            part = slice(64 * half, 64 * half + 64)
            both = dot(row[0, turn, part].reshape(256, 192), pair)
            extra = dot(row[1, turn, part].reshape(256, 192), h)
            total = (both[:, :128] + both[:, 128:] + extra).reshape(4, 8, 8, 128)
            total = (total - removed).reshape(4, 64, 128)
            if n:
                acc[half] += total
            else:
                acc[half] = total
            if n == 3 and half == 0:
                for i in (1, 0, 2, 3):
                    cross(i).start()

    for i in (1, 0, 2, 3):
        zq = near[i]
        cross(i).wait_recv()
        osend[i] = acc[1, zq] + part_in[i]
        for step in AROUND[0 if i else 1 :]:
            yq = lax.rem(y + step, 8)
            pltpu.make_async_remote_copy(
                src_ref=osend.at[i, pl.ds(yq * 8, 8)],
                dst_ref=orecv.at[z, pl.ds(y * 8, 8)],
                send_sem=osend_sem.at[i],
                recv_sem=orecv_sem.at[z],
                device_id={"slab": (zq * 8 + yq) * 2 + core},
            ).start()
        if i == 0:
            orecv[z, pl.ds(y * 8, 8)] = osend[i, pl.ds(y * 8, 8)]

    def lev_copy(n, side):
        return pltpu.make_async_remote_copy(
            src_ref=wsend.at[n],
            dst_ref=wrecv.at[side, n],
            send_sem=wsend_sem.at[side, n],
            recv_sem=wrecv_sem.at[side, n],
            device_id={"lev": lev + 1 if side == 0 else lev - 1},
        )

    @pl.when(even)
    def _():
        pl.semaphore_wait(level_sem, neighbours)

    for n in range(4):
        zs = near[n]
        size = 64 if n else 56
        pltpu.make_async_copy(orecv.at[zs, pl.ds(0, size)], orecv.at[zs, pl.ds(0, size)], orecv_sem.at[zs]).wait()
        tile = [orecv[zs, 8 * f : 8 * f + 8] + local[zs, f] for f in range(8)]
        lanes = pl.ds(pl.multiple_of(zs * 128, 128), 128)
        for f in range(4):
            out[f, :, lanes] = tile[f]
        for f, (a, b) in enumerate(PRODUCTS):
            flux = tile[4 + f] - tile[a] * tile[b]
            out[4 + f, :, lanes] = flux
            if f < 3:
                wsend[n, 8 * f : 8 * f + 8] = density[0] * flux

        @pl.when(has_up)
        def _(n=n):
            lev_copy(n, 0).start()

        @pl.when(has_down)
        def _(n=n):
            lev_copy(n, 1).start()

    @pl.when(jnp.logical_not(has_down))
    def _():
        wrecv[0] = jnp.zeros_like(wrecv[0])

    @pl.when(jnp.logical_not(has_up))
    def _():
        wrecv[1] = jnp.zeros_like(wrecv[1])

    for n, k in enumerate(ORDER):
        sent = send.at[n, pl.ds(0, 8 if k else 7), pl.ds(0, SENT)]
        pltpu.make_async_copy(sent, sent, send_sem.at[n]).wait()
        size = 64 if n else 56
        pltpu.make_async_copy(osend.at[n, pl.ds(0, size)], osend.at[n, pl.ds(0, size)], osend_sem.at[n]).wait()
        cross(n).wait_send()

    @pl.when(has_down)
    def _():
        for n in range(4):
            lev_copy(n, 1).wait_send()
            lev_copy(n, 0).wait_recv()

    @pl.when(has_up)
    def _():
        for n in range(4):
            lev_copy(n, 0).wait_send()
            lev_copy(n, 1).wait_recv()

    factor = thickness[0] / (2.0 * density[0])
    for n in range(4):
        lanes = pl.ds(pl.multiple_of(near[n] * 128, 128), 128)
        for f in range(3):
            rows = slice(8 * f, 8 * f + 8)
            out[8 + f, :, lanes] = -(wrecv[1, n, rows] - wrecv[0, n, rows]) * factor


def shards(columns, rows, fields, density, thickness):
    hbm = pl.BlockSpec(memory_space=pltpu.HBM)
    vmem = pl.BlockSpec(memory_space=pltpu.VMEM)
    dma = pltpu.SemaphoreType.DMA
    out = pl.pallas_call(
        kernel,
        out_shape=jax.ShapeDtypeStruct((11, 8, TARGET), F32),
        in_specs=[hbm] * 5,
        out_specs=vmem,
        scratch_shapes=[
            pltpu.SMEM((1,), F32),
            pltpu.SMEM((1,), F32),
            pltpu.VMEM((4, 32, GRID), F32),
            pltpu.VMEM((GRID, 128), F32),
            pltpu.VMEM((4, 128, 192), F32),
            pltpu.VMEM((GRID + 1536, 256), BF16),
            pltpu.VMEM((2, 7, 128, 192), BF16),
            pltpu.VMEM((256, GRID), BF16),
            pltpu.VMEM((256, GRID), BF16),
            pltpu.VMEM((256, 128), F32),
            pltpu.VMEM((4, 8, 32, 128), F32),
            pltpu.VMEM((4, 8, 32, 128), F32),
            pltpu.VMEM((4, 8, 8, 128), F32),
            pltpu.VMEM((2, 4, 64, 128), F32),
            pltpu.VMEM((4, 64, 128), F32),
            pltpu.VMEM((4, 64, 128), F32),
            pltpu.VMEM((4, 64, 128), F32),
            pltpu.VMEM((4, 24, 128), F32),
            pltpu.VMEM((2, 4, 24, 128), F32),
            dma((5,)),
            dma((4,)),
            dma((4,)),
            dma((2, 4)),
            dma((4,)),
            dma((4,)),
            dma((2, 4)),
            dma((2, 4)),
            pltpu.SemaphoreType.REGULAR,
        ],
        compiler_params=pltpu.CompilerParams(
            collective_id=0, has_side_effects=True, vmem_limit_bytes=54528 * 1024
        ),
    )(fields, density, thickness, columns, rows)
    return out[None, :4], out[None, 4:8], out[None, 8:]


def solution(mesh):
    columns, rows = tables()
    placed = P("lev", None, "slab", None)
    return jax.shard_map(
        functools.partial(shards, columns, rows),
        mesh=mesh,
        in_specs=(placed, P("lev"), P("lev")),
        out_specs=(placed, placed, placed),
        check_vma=False,
    )
```

```python
import functools

import jax
import jax.numpy as jnp
import ml_dtypes
import numpy as np
from jax import lax
from jax.experimental import pallas as pl
from jax.experimental.pallas import tpu as pltpu
from jax.sharding import PartitionSpec as P

GRID = 2048
TARGET = 512
SENT = 25
RELAYED = (0, 1)
ORDER = (2, 1, 3, 0)
PRODUCTS = ((0, 2), (1, 2), (3, 2), (0, 1))
AROUND = (0, 4, 1, 5, 2, 6, 3, 7)
NEAREST = ((0, 1, 2, 3), (1, 0, 2, 3), (2, 3, 1, 0), (3, 2, 1, 0))
F32 = jnp.float32
BF16 = jnp.bfloat16


def tables():
    k = np.arange(1, TARGET // 2, dtype=np.float64)
    offsets = np.arange(GRID, dtype=np.float64)
    profile = (1.0 + 2.0 * np.cos(2.0 * np.pi * np.outer(offsets, k) / GRID).sum(1)) / GRID
    index = (GRID // TARGET * np.arange(TARGET)[:, None] - np.arange(GRID)[None, :]) % GRID
    matrix = profile[index].astype(np.float32)
    columns = np.ascontiguousarray(matrix[:128].T)
    first = matrix[:, :512].reshape(4, 8, 2, 8, 8, 2, 8, 4)[..., 1:].swapaxes(6, 7)
    rows = [
        np.stack([first[:, :, c, :, :, core] for c in (1 - core, core)], axis=1).reshape(4, 128, 192)
        for core in range(2)
    ]
    return columns, np.stack(rows)


def split(value):
    high = value.astype(BF16)
    return high, (value - high.astype(F32)).astype(BF16)


def dot(a, b):
    return jnp.dot(a, b, preferred_element_type=F32)


def kernel(
    fields, density_hbm, thickness_hbm, col_hbm, row_hbm, out,
    density, thickness, g_in, col_in, row_in, col, row, g_high, g_low, whole, send, recv, local, acc, part_in, osend, orecv, wsend, wrecv,
    load_sem, send_sem, recv_sem, part_sem, osend_sem, orecv_sem, wsend_sem, wrecv_sem, relay_sem, level_sem,
):
    slab, lev = lax.axis_index("slab"), lax.axis_index("lev")
    core, chip = lax.rem(slab, 2), lax.div(slab, 2)
    z, y = lax.div(chip, 8), lax.rem(chip, 8)
    has_up, has_down = lev < 7, lev > 0
    even, odd = lax.rem(lev, 2) == 0, lax.rem(lev, 2) == 1
    neighbours = has_up.astype(jnp.int32) + has_down.astype(jnp.int32)
    near = [jnp.where(z < 2, jnp.where(z == 0, a, b), jnp.where(z == 2, c, d)) for a, b, c, d in zip(*NEAREST)]

    barrier = pltpu.get_barrier_semaphore()

    for i in reversed(range(4)):
        for step in AROUND[0 if i else 1 :]:
            peer = near[i] * 8 + lax.rem(y + step, 8)
            pl.semaphore_signal(barrier, inc=1, device_id={"slab": 2 * peer + core})
    pl.semaphore_signal(barrier, inc=1, device_id={"slab": 2 * chip + 1 - core})

    def greet_levels(semaphore):
        @pl.when(has_up)
        def _():
            pl.semaphore_signal(semaphore, inc=1, device_id={"lev": lev + 1})

        @pl.when(has_down)
        def _():
            pl.semaphore_signal(semaphore, inc=1, device_id={"lev": lev - 1})

    @pl.when(even)
    def _():
        greet_levels(barrier)

    load = pltpu.make_async_copy(fields.at[0], g_in, load_sem.at[0])
    load.start()
    col_load = pltpu.make_async_copy(col_hbm, col_in, load_sem.at[1])
    col_load.start()
    row_load = pltpu.make_async_copy(row_hbm.at[core], row_in, load_sem.at[2])
    row_load.start()
    scalars = [
        pltpu.make_async_copy(density_hbm, density, load_sem.at[3]),
        pltpu.make_async_copy(thickness_hbm, thickness, load_sem.at[4]),
    ]
    for c in scalars:
        c.start()

    load.wait()
    fine = [g_in[f] for f in range(4)]
    fine += [fine[a] * fine[b] for a, b in PRODUCTS]
    for f in range(8):
        h, l = split(fine[f])
        g_high[32 * f : 32 * f + 32] = h
        g_low[32 * f : 32 * f + 32] = l

    col_load.wait()
    h, l = split(col_in[...])
    col[:GRID, :128], col[:GRID, 128:] = h, l
    col[GRID:, :128], col[GRID:, 128:] = h[:1536], l[:1536]

    alternating = 1.0 - 2.0 * lax.rem(lax.broadcasted_iota(jnp.int32, (8, 128), 0), 2).astype(F32)
    for n, k in enumerate(ORDER):
        zq = lax.rem(z + k, 4)
        turn = pl.ds(pl.multiple_of(512 * lax.rem(4 - zq, 4), 512), GRID)
        both = dot(g_high[...], col[turn])
        extra = dot(g_low[...], col[turn, :128])
        whole[...] = both[:, :128] + both[:, 128:] + extra
        for f in range(8):
            for s in (1, 2, 3):
                send[n, f, 8 * s - 8 : 8 * s] = whole[pl.ds(32 * f + s, 8, 4)]
            kept = whole[pl.ds(32 * f, 8, 4)]
            send[n, f, 24:25] = jnp.sum(kept * alternating, axis=0, keepdims=True)
            local[zq, f] = 0.25 * kept
        if n == 0:
            pl.semaphore_wait(barrier, 32 + jnp.where(even, 0, neighbours))

            @pl.when(jnp.logical_not(even))
            def _():
                greet_levels(level_sem)


        for step in AROUND[0 if k else 1 :]:
            yq = lax.rem(y + step, 8)
            pltpu.make_async_remote_copy(
                src_ref=send.at[n, yq, pl.ds(0, SENT)],
                dst_ref=recv.at[z, y, pl.ds(0, SENT)],
                send_sem=send_sem.at[n],
                recv_sem=recv_sem.at[z],
                device_id={"slab": (zq * 8 + yq) * 2 + core},
            ).start()
        if k == 0:
            recv[z, y] = send[n, y]

    row_load.wait()
    for c in scalars:
        c.wait()
    h, l = split(row_in[...])
    row[0, :4], row[1, :4] = h, l
    row[0, 4:], row[1, 4:] = h[:3], l[:3]

    def cross(i):
        return pltpu.make_async_remote_copy(
            src_ref=acc.at[0, near[i]],
            dst_ref=part_in.at[i],
            send_sem=part_sem.at[0, i],
            recv_sem=part_sem.at[1, i],
            device_id={"slab": 2 * chip + 1 - core},
        )

    for n, k in enumerate(ORDER):
        zs = lax.rem(z + 4 - k, 4)
        arrived = recv.at[zs, pl.ds(0, 8 if k else 7), pl.ds(0, SENT)]
        pltpu.make_async_copy(arrived, arrived, recv_sem.at[zs]).wait()
        h, l = split(recv[zs, :, :24].reshape(192, 128))
        removed = jnp.sum(recv[zs, :, 24], axis=0, keepdims=True) * alternating * (1.0 / GRID)
        turn = pl.ds(lax.rem(4 - zs, 4), 4)
        pair = jnp.concatenate([h, l], axis=1)
        for half in range(2):
            part = slice(64 * half, 64 * half + 64)
            both = dot(row[0, turn, part].reshape(256, 192), pair)
            extra = dot(row[1, turn, part].reshape(256, 192), h)
            total = (both[:, :128] + both[:, 128:] + extra).reshape(4, 8, 8, 128)
            total = (total - removed).reshape(4, 64, 128)
            if n:
                acc[half] += total
            else:
                acc[half] = total
            if n == 3 and half == 0:
                for i in (1, 0, 2, 3):
                    cross(i).start()

    for i in (1, 0, 2, 3):
        zq = near[i]
        cross(i).wait_recv()
        osend[i] = acc[1, zq] + part_in[i]
        for step in AROUND[0 if i else 1 :]:
            yq = lax.rem(y + step, 8)
            pltpu.make_async_remote_copy(
                src_ref=osend.at[i, pl.ds(yq * 8, 8)],
                dst_ref=orecv.at[z, pl.ds(y * 8, 8)],
                send_sem=osend_sem.at[i],
                recv_sem=orecv_sem.at[z],
                device_id={"slab": (zq * 8 + yq) * 2 + core},
            ).start()
        if i == 0:
            orecv[z, pl.ds(y * 8, 8)] = osend[i, pl.ds(y * 8, 8)]

    def lev_copy(n, side):
        return pltpu.make_async_remote_copy(
            src_ref=wsend.at[n],
            dst_ref=wrecv.at[side, n],
            send_sem=wsend_sem.at[side, n],
            recv_sem=wrecv_sem.at[side, n],
            device_id={"lev": lev + 1 if side == 0 else lev - 1},
        )

    @pl.when(even)
    def _():
        pl.semaphore_wait(level_sem, neighbours)

    for n in range(4):
        zs = near[n]
        size = 64 if n else 56
        pltpu.make_async_copy(orecv.at[zs, pl.ds(0, size)], orecv.at[zs, pl.ds(0, size)], orecv_sem.at[zs]).wait()
        tile = [orecv[zs, 8 * f : 8 * f + 8] + local[zs, f] for f in range(8)]
        lanes = pl.ds(pl.multiple_of(zs * 128, 128), 128)
        for f in range(4):
            out[f, :, lanes] = tile[f]
        for f, (a, b) in enumerate(PRODUCTS):
            flux = tile[4 + f] - tile[a] * tile[b]
            out[4 + f, :, lanes] = flux
            if f < 3:
                wsend[n, 8 * f : 8 * f + 8] = density[0] * flux

        @pl.when(even if n in RELAYED else has_up)
        def _(n=n):
            lev_copy(n, 0).start()

        @pl.when(odd if n in RELAYED else has_down)
        def _(n=n):
            lev_copy(n, 1).start()

    def relay(n, side):
        return pltpu.make_async_remote_copy(
            src_ref=wrecv.at[1 - side, n],
            dst_ref=wrecv.at[side, n],
            send_sem=relay_sem.at[n],
            recv_sem=wrecv_sem.at[side, n],
            device_id={"lev": lev + 2 if side == 0 else lev - 2},
        )

    for mine, side, has_next in ((even, 0, lev < 6), (odd, 1, lev > 1)):

        @pl.when(mine)
        def _(side=side, has_next=has_next):
            for n in RELAYED:
                lev_copy(n, 1 - side).wait_recv()

                @pl.when(has_next)
                def _(n=n):
                    relay(n, side).start()

    @pl.when(jnp.logical_not(has_down))
    def _():
        wrecv[0] = jnp.zeros_like(wrecv[0])

    @pl.when(jnp.logical_not(has_up))
    def _():
        wrecv[1] = jnp.zeros_like(wrecv[1])

    for n, k in enumerate(ORDER):
        sent = send.at[n, pl.ds(0, 8 if k else 7), pl.ds(0, SENT)]
        pltpu.make_async_copy(sent, sent, send_sem.at[n]).wait()
        size = 64 if n else 56
        pltpu.make_async_copy(osend.at[n, pl.ds(0, size)], osend.at[n, pl.ds(0, size)], osend_sem.at[n]).wait()
        cross(n).wait_send()

    for mine, side, has_next, has_other in ((even, 0, lev < 6, has_down), (odd, 1, lev > 1, has_up)):

        @pl.when(mine)
        def _(side=side, has_next=has_next, has_other=has_other):
            for n in range(4):
                lev_copy(n, side).wait_send()
                if n not in RELAYED:
                    lev_copy(n, 1 - side).wait_recv()

            @pl.when(has_other)
            def _():
                for n in range(4):
                    if n not in RELAYED:
                        lev_copy(n, 1 - side).wait_send()
                    lev_copy(n, side).wait_recv()

            @pl.when(has_next)
            def _():
                for n in RELAYED:
                    relay(n, side).wait_send()

    factor = thickness[0] / (2.0 * density[0])
    for n in range(4):
        lanes = pl.ds(pl.multiple_of(near[n] * 128, 128), 128)
        for f in range(3):
            rows = slice(8 * f, 8 * f + 8)
            out[8 + f, :, lanes] = -(wrecv[1, n, rows] - wrecv[0, n, rows]) * factor


def shards(columns, rows, fields, density, thickness):
    hbm = pl.BlockSpec(memory_space=pltpu.HBM)
    vmem = pl.BlockSpec(memory_space=pltpu.VMEM)
    dma = pltpu.SemaphoreType.DMA
    out = pl.pallas_call(
        kernel,
        out_shape=jax.ShapeDtypeStruct((11, 8, TARGET), F32),
        in_specs=[hbm] * 5,
        out_specs=vmem,
        scratch_shapes=[
            pltpu.SMEM((1,), F32),
            pltpu.SMEM((1,), F32),
            pltpu.VMEM((4, 32, GRID), F32),
            pltpu.VMEM((GRID, 128), F32),
            pltpu.VMEM((4, 128, 192), F32),
            pltpu.VMEM((GRID + 1536, 256), BF16),
            pltpu.VMEM((2, 7, 128, 192), BF16),
            pltpu.VMEM((256, GRID), BF16),
            pltpu.VMEM((256, GRID), BF16),
            pltpu.VMEM((256, 128), F32),
            pltpu.VMEM((4, 8, 32, 128), F32),
            pltpu.VMEM((4, 8, 32, 128), F32),
            pltpu.VMEM((4, 8, 8, 128), F32),
            pltpu.VMEM((2, 4, 64, 128), F32),
            pltpu.VMEM((4, 64, 128), F32),
            pltpu.VMEM((4, 64, 128), F32),
            pltpu.VMEM((4, 64, 128), F32),
            pltpu.VMEM((4, 24, 128), F32),
            pltpu.VMEM((2, 4, 24, 128), F32),
            dma((5,)),
            dma((4,)),
            dma((4,)),
            dma((2, 4)),
            dma((4,)),
            dma((4,)),
            dma((2, 4)),
            dma((2, 4)),
            dma((4,)),
            pltpu.SemaphoreType.REGULAR,
        ],
        compiler_params=pltpu.CompilerParams(
            collective_id=0, has_side_effects=True, vmem_limit_bytes=54528 * 1024
        ),
    )(fields, density, thickness, columns, rows)
    return out[None, :4], out[None, 4:8], out[None, 8:]


def solution(mesh):
    columns, rows = tables()
    placed = P("lev", None, "slab", None)
    return jax.shard_map(
        functools.partial(shards, columns, rows),
        mesh=mesh,
        in_specs=(placed, P("lev"), P("lev")),
        out_specs=(placed, placed, placed),
        check_vma=False,
    )
```

```python
import functools

import jax
import jax.numpy as jnp
import ml_dtypes
import numpy as np
from jax import lax
from jax.experimental import pallas as pl
from jax.experimental.pallas import tpu as pltpu
from jax.sharding import PartitionSpec as P

GRID = 2048
TARGET = 512
SENT = 25
RELAYED = (0, 1)
ORDER = (2, 1, 3, 0)
PRODUCTS = ((0, 2), (1, 2), (3, 2), (0, 1))
AROUND = (0, 4, 1, 5, 2, 6, 3, 7)
NEAREST = ((0, 1, 2, 3), (1, 0, 2, 3), (2, 3, 1, 0), (3, 2, 1, 0))
F32 = jnp.float32
BF16 = jnp.bfloat16


def tables():
    k = np.arange(1, TARGET // 2, dtype=np.float64)
    offsets = np.arange(GRID, dtype=np.float64)
    profile = (1.0 + 2.0 * np.cos(2.0 * np.pi * np.outer(offsets, k) / GRID).sum(1)) / GRID
    index = (GRID // TARGET * np.arange(TARGET)[:, None] - np.arange(GRID)[None, :]) % GRID
    matrix = profile[index].astype(np.float32)
    columns = np.ascontiguousarray(matrix[:, :512].T)
    first = matrix[:, :512].reshape(4, 8, 2, 8, 8, 2, 8, 4)[..., 1:].swapaxes(6, 7)
    rows = [
        np.stack([first[:, :, c, :, :, core] for c in (1 - core, core)], axis=1).reshape(4, 128, 192)
        for core in range(2)
    ]
    return columns, np.stack(rows)


def split(value):
    high = value.astype(BF16)
    return high, (value - high.astype(F32)).astype(BF16)


def dot(a, b):
    return jnp.dot(a, b, preferred_element_type=F32)


def kernel(
    fields, density_hbm, thickness_hbm, col_hbm, row_hbm, out,
    density, thickness, g_in, col_in, row_in, col, row, g_high, g_low, whole, send, recv, local, acc, part_in, osend, orecv, wsend, wrecv,
    load_sem, send_sem, recv_sem, part_sem, osend_sem, orecv_sem, wsend_sem, wrecv_sem, relay_sem, level_sem,
):
    slab, lev = lax.axis_index("slab"), lax.axis_index("lev")
    core, chip = lax.rem(slab, 2), lax.div(slab, 2)
    z, y = lax.div(chip, 8), lax.rem(chip, 8)
    has_up, has_down = lev < 7, lev > 0
    even, odd = lax.rem(lev, 2) == 0, lax.rem(lev, 2) == 1
    neighbours = has_up.astype(jnp.int32) + has_down.astype(jnp.int32)
    near = [jnp.where(z < 2, jnp.where(z == 0, a, b), jnp.where(z == 2, c, d)) for a, b, c, d in zip(*NEAREST)]

    loads = [pltpu.make_async_copy(fields.at[0, f], g_in.at[f], load_sem.at[f]) for f in range(4)]
    loads.append(pltpu.make_async_copy(col_hbm.at[pl.ds(0, 8)], col_in, load_sem.at[4]))
    for c in reversed(loads):
        c.start()
    barrier = pltpu.get_barrier_semaphore()

    for i in reversed(range(4)):
        for step in AROUND[0 if i else 1 :]:
            peer = near[i] * 8 + lax.rem(y + step, 8)
            pl.semaphore_signal(barrier, inc=1, device_id={"slab": 2 * peer + core})
    pl.semaphore_signal(barrier, inc=1, device_id={"slab": 2 * chip + 1 - core})

    def greet_levels(semaphore):
        @pl.when(has_up)
        def _():
            pl.semaphore_signal(semaphore, inc=1, device_id={"lev": lev + 1})

        @pl.when(has_down)
        def _():
            pl.semaphore_signal(semaphore, inc=1, device_id={"lev": lev - 1})

    @pl.when(even)
    def _():
        greet_levels(barrier)

    loads[4].wait()
    lane = lax.broadcasted_iota(jnp.int32, (8, 128), 1)
    for shift in range(0, 128, 4):
        for q in range(4):
            pair = []
            for turn in (shift, shift + 2):
                here = col_in[:, 128 * q : 128 * q + 128]
                if turn:
                    before = col_in[:, 128 * ((q + 3) % 4) : 128 * ((q + 3) % 4) + 128]
                    here = jnp.where(lane < turn, pltpu.roll(before, turn, 1), pltpu.roll(here, turn, 1))
                pair.append(here)
            h, l = split(jnp.concatenate(pair))
            at = 512 * ((4 - q) % 4) + 4 * shift
            col[at : at + 16, :128], col[at : at + 16, 128:] = h, l
            if at < 1536:
                col[GRID + at : GRID + at + 16, :128], col[GRID + at : GRID + at + 16, 128:] = h, l
    for c in loads[:4]:
        c.wait()
    fine = [g_in[f] for f in range(4)]
    fine += [fine[a] * fine[b] for a, b in PRODUCTS]
    for f in range(8):
        h, l = split(fine[f])
        g_high[32 * f : 32 * f + 32] = h
        g_low[32 * f : 32 * f + 32] = l

    row_load = pltpu.make_async_copy(row_hbm.at[core], row_in, load_sem.at[8])
    row_load.start()
    scalars = [
        pltpu.make_async_copy(density_hbm, density, load_sem.at[9]),
        pltpu.make_async_copy(thickness_hbm, thickness, load_sem.at[10]),
    ]
    for c in scalars:
        c.start()

    alternating = 1.0 - 2.0 * lax.rem(lax.broadcasted_iota(jnp.int32, (8, 128), 0), 2).astype(F32)
    for n, k in enumerate(ORDER):
        zq = lax.rem(z + k, 4)
        turn = pl.ds(pl.multiple_of(512 * lax.rem(4 - zq, 4), 512), GRID)
        both = dot(g_high[...], col[turn])
        extra = dot(g_low[...], col[turn, :128])
        whole[...] = both[:, :128] + both[:, 128:] + extra
        for f in range(8):
            for s in (1, 2, 3):
                send[n, f, 8 * s - 8 : 8 * s] = whole[pl.ds(32 * f + s, 8, 4)]
            kept = whole[pl.ds(32 * f, 8, 4)]
            send[n, f, 24:25] = jnp.sum(kept * alternating, axis=0, keepdims=True)
            local[zq, f] = 0.25 * kept

    pl.semaphore_wait(barrier, 32 + jnp.where(even, 0, neighbours))

    @pl.when(jnp.logical_not(even))
    def _():
        greet_levels(level_sem)

    for n, k in enumerate(ORDER):
        zq = lax.rem(z + k, 4)
        for step in AROUND[0 if k else 1 :]:
            yq = lax.rem(y + step, 8)
            pltpu.make_async_remote_copy(
                src_ref=send.at[n, yq, pl.ds(0, SENT)],
                dst_ref=recv.at[z, y, pl.ds(0, SENT)],
                send_sem=send_sem.at[n],
                recv_sem=recv_sem.at[z],
                device_id={"slab": (zq * 8 + yq) * 2 + core},
            ).start()
        if k == 0:
            recv[z, y] = send[n, y]

    row_load.wait()
    for c in scalars:
        c.wait()
    h, l = split(row_in[...])
    row[0, :4], row[1, :4] = h, l
    row[0, 4:], row[1, 4:] = h[:3], l[:3]

    def cross(i):
        return pltpu.make_async_remote_copy(
            src_ref=acc.at[0, near[i]],
            dst_ref=part_in.at[i],
            send_sem=part_sem.at[0, i],
            recv_sem=part_sem.at[1, i],
            device_id={"slab": 2 * chip + 1 - core},
        )

    for n, k in enumerate(ORDER):
        zs = lax.rem(z + 4 - k, 4)
        arrived = recv.at[zs, pl.ds(0, 8 if k else 7), pl.ds(0, SENT)]
        pltpu.make_async_copy(arrived, arrived, recv_sem.at[zs]).wait()
        h, l = split(recv[zs, :, :24].reshape(192, 128))
        removed = jnp.sum(recv[zs, :, 24], axis=0, keepdims=True) * alternating * (1.0 / GRID)
        turn = pl.ds(lax.rem(4 - zs, 4), 4)
        pair = jnp.concatenate([h, l], axis=1)
        for half in range(2):
            part = slice(64 * half, 64 * half + 64)
            both = dot(row[0, turn, part].reshape(256, 192), pair)
            extra = dot(row[1, turn, part].reshape(256, 192), h)
            total = (both[:, :128] + both[:, 128:] + extra).reshape(4, 8, 8, 128)
            total = (total - removed).reshape(4, 64, 128)
            if n:
                acc[half] += total
            else:
                acc[half] = total
            if n == 3 and half == 0:
                for i in (1, 0, 2, 3):
                    cross(i).start()

    for i in (1, 0, 2, 3):
        zq = near[i]
        cross(i).wait_recv()
        osend[i] = acc[1, zq] + part_in[i]
        for step in AROUND[0 if i else 1 :]:
            yq = lax.rem(y + step, 8)
            pltpu.make_async_remote_copy(
                src_ref=osend.at[i, pl.ds(yq * 8, 8)],
                dst_ref=orecv.at[z, pl.ds(y * 8, 8)],
                send_sem=osend_sem.at[i],
                recv_sem=orecv_sem.at[z],
                device_id={"slab": (zq * 8 + yq) * 2 + core},
            ).start()
        if i == 0:
            orecv[z, pl.ds(y * 8, 8)] = osend[i, pl.ds(y * 8, 8)]

    def lev_copy(n, side):
        return pltpu.make_async_remote_copy(
            src_ref=wsend.at[n],
            dst_ref=wrecv.at[side, n],
            send_sem=wsend_sem.at[side, n],
            recv_sem=wrecv_sem.at[side, n],
            device_id={"lev": lev + 1 if side == 0 else lev - 1},
        )

    @pl.when(even)
    def _():
        pl.semaphore_wait(level_sem, neighbours)

    for n in range(4):
        zs = near[n]
        size = 64 if n else 56
        pltpu.make_async_copy(orecv.at[zs, pl.ds(0, size)], orecv.at[zs, pl.ds(0, size)], orecv_sem.at[zs]).wait()
        tile = [orecv[zs, 8 * f : 8 * f + 8] + local[zs, f] for f in range(8)]
        lanes = pl.ds(pl.multiple_of(zs * 128, 128), 128)
        for f in range(4):
            out[f, :, lanes] = tile[f]
        for f, (a, b) in enumerate(PRODUCTS):
            flux = tile[4 + f] - tile[a] * tile[b]
            out[4 + f, :, lanes] = flux
            if f < 3:
                wsend[n, 8 * f : 8 * f + 8] = density[0] * flux

        @pl.when(even if n in RELAYED else has_up)
        def _(n=n):
            lev_copy(n, 0).start()

        @pl.when(odd if n in RELAYED else has_down)
        def _(n=n):
            lev_copy(n, 1).start()

    def relay(n, side):
        return pltpu.make_async_remote_copy(
            src_ref=wrecv.at[1 - side, n],
            dst_ref=wrecv.at[side, n],
            send_sem=relay_sem.at[n],
            recv_sem=wrecv_sem.at[side, n],
            device_id={"lev": lev + 2 if side == 0 else lev - 2},
        )

    for mine, side, has_next in ((even, 0, lev < 6), (odd, 1, lev > 1)):

        @pl.when(mine)
        def _(side=side, has_next=has_next):
            for n in RELAYED:
                lev_copy(n, 1 - side).wait_recv()

                @pl.when(has_next)
                def _(n=n):
                    relay(n, side).start()

    @pl.when(jnp.logical_not(has_down))
    def _():
        wrecv[0] = jnp.zeros_like(wrecv[0])

    @pl.when(jnp.logical_not(has_up))
    def _():
        wrecv[1] = jnp.zeros_like(wrecv[1])

    for n, k in enumerate(ORDER):
        sent = send.at[n, pl.ds(0, 8 if k else 7), pl.ds(0, SENT)]
        pltpu.make_async_copy(sent, sent, send_sem.at[n]).wait()
        size = 64 if n else 56
        pltpu.make_async_copy(osend.at[n, pl.ds(0, size)], osend.at[n, pl.ds(0, size)], osend_sem.at[n]).wait()
        cross(n).wait_send()

    for mine, side, has_next, has_other in ((even, 0, lev < 6, has_down), (odd, 1, lev > 1, has_up)):

        @pl.when(mine)
        def _(side=side, has_next=has_next, has_other=has_other):
            for n in range(4):
                lev_copy(n, side).wait_send()
                if n not in RELAYED:
                    lev_copy(n, 1 - side).wait_recv()

            @pl.when(has_other)
            def _():
                for n in range(4):
                    if n not in RELAYED:
                        lev_copy(n, 1 - side).wait_send()
                    lev_copy(n, side).wait_recv()

            @pl.when(has_next)
            def _():
                for n in RELAYED:
                    relay(n, side).wait_send()

    factor = thickness[0] / (2.0 * density[0])
    for n in range(4):
        lanes = pl.ds(pl.multiple_of(near[n] * 128, 128), 128)
        for f in range(3):
            rows = slice(8 * f, 8 * f + 8)
            out[8 + f, :, lanes] = -(wrecv[1, n, rows] - wrecv[0, n, rows]) * factor


def shards(columns, rows, fields, density, thickness):
    hbm = pl.BlockSpec(memory_space=pltpu.HBM)
    vmem = pl.BlockSpec(memory_space=pltpu.VMEM)
    dma = pltpu.SemaphoreType.DMA
    out = pl.pallas_call(
        kernel,
        out_shape=jax.ShapeDtypeStruct((11, 8, TARGET), F32),
        in_specs=[hbm] * 5,
        out_specs=vmem,
        scratch_shapes=[
            pltpu.SMEM((1,), F32),
            pltpu.SMEM((1,), F32),
            pltpu.VMEM((4, 32, GRID), F32),
            pltpu.VMEM((8, 512), F32),
            pltpu.VMEM((4, 128, 192), F32),
            pltpu.VMEM((GRID + 1536, 256), BF16),
            pltpu.VMEM((2, 7, 128, 192), BF16),
            pltpu.VMEM((256, GRID), BF16),
            pltpu.VMEM((256, GRID), BF16),
            pltpu.VMEM((256, 128), F32),
            pltpu.VMEM((4, 8, 32, 128), F32),
            pltpu.VMEM((4, 8, 32, 128), F32),
            pltpu.VMEM((4, 8, 8, 128), F32),
            pltpu.VMEM((2, 4, 64, 128), F32),
            pltpu.VMEM((4, 64, 128), F32),
            pltpu.VMEM((4, 64, 128), F32),
            pltpu.VMEM((4, 64, 128), F32),
            pltpu.VMEM((4, 24, 128), F32),
            pltpu.VMEM((2, 4, 24, 128), F32),
            dma((11,)),
            dma((4,)),
            dma((4,)),
            dma((2, 4)),
            dma((4,)),
            dma((4,)),
            dma((2, 4)),
            dma((2, 4)),
            dma((4,)),
            pltpu.SemaphoreType.REGULAR,
        ],
        compiler_params=pltpu.CompilerParams(
            collective_id=0, has_side_effects=True, vmem_limit_bytes=54528 * 1024
        ),
    )(fields, density, thickness, columns, rows)
    return out[None, :4], out[None, 4:8], out[None, 8:]


def solution(mesh):
    columns, rows = tables()
    placed = P("lev", None, "slab", None)
    return jax.shard_map(
        functools.partial(shards, columns, rows),
        mesh=mesh,
        in_specs=(placed, P("lev"), P("lev")),
        out_specs=(placed, placed, placed),
        check_vma=False,
    )
```
